32 devices in a mesh: groups: 2 (over y), ctx: 4 (over x, core), head: 4 (over z).
Axes of the slice: x: 2, y: 2, z: 4, core: 2. Of those that a mesh axis runs over, the one named last changes fastest.
Arguments:
- queries: bfloat16 [1536, 8, 5, 128], P(('groups', 'ctx'), 'head'), parts along dimension 0, may hold values from -6 to 6
- keys_values: bfloat16 [1536, 8, 2, 128], P(('groups', 'ctx'), 'head'), parts along dimension 0, may hold values from -6 to 6
- prior_state: bfloat16 [16, 8256, 128], P(('groups', 'head'), 'ctx'), parts along dimension 0, may hold values from -224 to 224
- counts: int32 [2], P('groups'), parts along dimension 0, may hold values from 384 to 1535
- continuation: int32 [64], P('groups'), parts along dimension 0, may hold values from 0 to 75967
- query_table: bfloat16 [75968, 8, 5, 128], P('ctx', 'head'), may hold values from -6 to 6
- pair_table: bfloat16 [75968, 8, 2, 128], P('ctx', 'head'), may hold values from -6 to 6
Outputs:
- readout: bfloat16 [1536, 8, 5, 128], P(('groups', 'ctx'), 'head'), parts along dimension 0
- decode_out: bfloat16 [64, 8, 5, 128], P(('groups', 'ctx'), 'head'), parts along dimension 0
- decode_state: float32 [16, 8256, 128], P(('groups', 'head'), 'ctx'), parts along dimension 0
The draws below stay inside these ranges and needn't reach their ends.
There are 2 independent parts, one for each index of `groups`. The reference program is written for one: setup_inputs(seed, part) draws one part's arguments, and reference() takes and returns one part's arrays. A program takes and returns all parts, laid end to end along the dimension named above; an argument that names none is the same for every part. Nothing has to cross between parts.
All inputs are finite; a program needn't handle non-finite values.
Results may differ from the reference program's by a relative error of at most 0.0048.
The reference program's roundings to bfloat16 on the way count: a program that leaves them out, or rounds other values in their place, can miss the bound.
Values may be sent and summed in bfloat16 or wider, within the bound.
No kernel may reach another device: no remote copies, remote signals or barrier semaphores. Data moves between devices by JAX's collectives and lax.ppermute only.
A program may use at most 256 MiB of HBM per device.

```python
import math
import jax
import jax.numpy as jnp
import numpy as np
from jax import lax

HD = 128
KV = 8
G = 5
DX = 8256
TOK_DEV = 192
TOKENS = 768
STEPS = 32
VOCAB = 75968


def with_ends(values, key, smallest, high):
    dims = values.shape
    spot = [jax.random.randint(jax.random.fold_in(key, axis), (), 0, dims[axis]) for axis in range(len(dims))]
    values = values.at[tuple(spot)].set(smallest)
    longest = dims.index(max(dims))
    spot[longest] = (spot[longest] + 1) % dims[longest]
    return values.at[tuple(spot)].set(high)


def block_scale(rng, shape, cuts, smallest, largest):
    level, own = 1.0, jax.random.fold_in(rng, 6)
    for axis_at, shards_of in cuts:
        draws = jnp.exp(jax.random.uniform(jax.random.fold_in(own, axis_at), (shards_of,), jnp.float32, smallest / len(cuts), largest / len(cuts)))
        level = level * jnp.repeat(draws, shape[axis_at] // shards_of).reshape([-1 if axis == axis_at else 1 for axis in range(len(shape))])
    return level


def ranked_wide(own_key, shape, count, skew):
    loads = [min(1 << octave, count + 1 - (1 << octave)) * (1 << 20) // math.isqrt((1 << octave) ** skew) + 1 for octave in range((count + 1).bit_length()) if 1 << octave <= count]
    spread = 1 + sum(loads) // (1 << 30)
    grid = np.cumsum(np.array([max(1, weight // spread) for weight in loads]))
    pick = jax.random.randint(jax.random.fold_in(own_key, 1), shape, 0, int(grid[len(loads) - 1]))
    start = jnp.left_shift(1, jnp.searchsorted(jnp.asarray(grid, jnp.int32), pick, side="right").astype(jnp.int32))
    rank = start - 1 + jax.random.randint(jax.random.fold_in(own_key, 4), shape, 0, 1 << 30) % jnp.minimum(start, count + 1 - start)
    return jax.random.permutation(jax.random.fold_in(own_key, 2), count)[rank].astype(jnp.int32)


def centred(key, shape, scale, bound, shards=(), held_as=jnp.bfloat16):
    result = jax.random.normal(key, shape, jnp.float32) * scale
    if len(shards) > 0:
        result = block_scale(key, shape, shards, -0.22, 0.18) * result
    return jnp.clip(result, min=-bound, max=bound).astype(held_as)


def setup_inputs(seed: int = 0, part: int = 0) -> dict:
    keys = jax.random.split(jax.random.key(seed), 8)
    part_splits = jax.random.split(jax.random.fold_in(keys[7], part), 8)
    queries = centred(part_splits[0], (TOKENS, KV, G, HD), 1.0, 6.0, ((0, 4), (1, 4)))
    keys_values = centred(part_splits[1], (TOKENS, KV, 2, HD), 1.0, 6.0, ((0, 4), (1, 4)))
    prior_state = centred(part_splits[2], (KV, DX, HD), ((2 * TOKENS) ** 0.5), 224.0, ((0, 4), (1, 4)))
    counts = jax.random.randint(part_splits[3], (1,), TOKENS // 2, 2 * TOKENS).astype(jnp.int32)
    continuation = with_ends(ranked_wide(part_splits[4], (STEPS,), VOCAB, 2), jax.random.fold_in(part_splits[4], 3), 0, VOCAB - 1).astype(jnp.int32)
    query_table = centred(keys[5], (VOCAB, KV, G, HD), 1.0, 6.0, ((0, 4), (1, 4)))
    pair_table = centred(keys[6], (VOCAB, KV, 2, HD), 1.0, 6.0, ((0, 4), (1, 4)))
    return {"queries": queries, "keys_values": keys_values, "prior_state": prior_state, "counts": counts, "continuation": continuation, "query_table": query_table, "pair_table": pair_table}


ROOT_TWO = 2.0 ** 0.5
NUM_BLOCKS = 8

def expand_range(values, first_offset, how_many):
    width = values.shape[-1]
    doubled = jnp.concatenate([values, values], axis=-1)
    scaled = doubled * ROOT_TWO
    pieces = []
    for offset in range(first_offset, first_offset + how_many):
        partner = doubled if offset == 0 else scaled
        pieces.append(values * partner[..., offset:offset + width])
    return jnp.concatenate(pieces, axis=-1)

def expand_tail(values):
    half_width = values.shape[-1] // 2
    return values[..., :half_width] * (values[..., half_width:] * ROOT_TWO)

def feature_piece(values, number):
    head_size = values.shape[-1]
    if number == NUM_BLOCKS:
        return expand_tail(values)
    per_block = head_size // 2 // NUM_BLOCKS
    return expand_range(values, number * per_block, per_block)

def expand_all(values):
    return jnp.concatenate([feature_piece(values, number) for number in range(NUM_BLOCKS + 1)], axis=-1)

def causal_sum(query_rows, key_rows, value_rows):
    scores = jnp.einsum('tgd,sd->gts', query_rows.astype(jnp.float32), key_rows.astype(jnp.float32))
    allowed = jnp.arange(query_rows.shape[0], dtype=jnp.int32)[:, None] >= jnp.arange(key_rows.shape[0], dtype=jnp.int32)[None, :]
    weights = jnp.where(allowed[None], scores * scores / HD, 0.0).astype(jnp.bfloat16)
    return jnp.einsum('gts,sd->tgd', weights.astype(jnp.float32), value_rows.astype(jnp.float32))

def head_window(packed, start_count):
    head_queries, head_pairs, head_prior, step_queries, step_pairs = packed
    block_queries_all = head_queries.reshape(-1, TOK_DEV, G, HD)
    block_pairs_all = head_pairs.reshape(-1, TOK_DEV, 2, HD)
    block_count = block_queries_all.shape[0]

    def advance(running, block):
        block_queries, block_pairs, block_number = block
        phi_keys = expand_all(block_pairs[:, 0].astype(jnp.float32)).astype(jnp.bfloat16)
        phi_queries = expand_all(block_queries.astype(jnp.float32)).astype(jnp.bfloat16)
        carried = jnp.dot(phi_queries.reshape(-1, DX), running.astype(jnp.bfloat16), preferred_element_type=jnp.float32).reshape(TOK_DEV, G, HD)
        own_sum = causal_sum(block_queries, block_pairs[:, 0], block_pairs[:, 1])
        positions = start_count + block_number * TOK_DEV + jnp.arange(TOK_DEV, dtype=jnp.int32) + 1
        output = ((carried / HD + own_sum) / jnp.sqrt(positions.astype(jnp.float32))[:, None, None]).astype(jnp.bfloat16)
        running = running + jnp.dot(phi_keys.T, block_pairs[:, 1], preferred_element_type=jnp.float32)
        return (running, output)
    final_state, outputs = lax.scan(advance, head_prior.astype(jnp.float32), (block_queries_all, block_pairs_all, jnp.arange(block_count, dtype=jnp.int32)))
    readout = outputs.reshape(TOKENS, G, HD)
    step_phi_queries = expand_all(step_queries.astype(jnp.float32)).astype(jnp.bfloat16)
    step_carried = jnp.dot(step_phi_queries.reshape(-1, DX), final_state.astype(jnp.bfloat16), preferred_element_type=jnp.float32).reshape(STEPS, G, HD)
    step_own = causal_sum(step_queries, step_pairs[:, 0], step_pairs[:, 1])
    step_positions = start_count + TOKENS + jnp.arange(STEPS, dtype=jnp.int32) + 1
    decode_out = ((step_carried / HD + step_own) / jnp.sqrt(step_positions.astype(jnp.float32))[:, None, None]).astype(jnp.bfloat16)
    step_phi_keys = expand_all(step_pairs[:, 0].astype(jnp.float32)).astype(jnp.bfloat16)
    decode_state = final_state + jnp.dot(step_phi_keys.T, step_pairs[:, 1], preferred_element_type=jnp.float32)
    return (readout, decode_out, decode_state)

def reference(queries, keys_values, prior_state, counts, continuation, query_table, pair_table):
    step_queries = jnp.take(query_table, continuation, axis=0)
    step_pairs = jnp.take(pair_table, continuation, axis=0)
    start_count = counts[0]

    def per_head(packed):
        return head_window(packed, start_count)
    readout, decode_out, decode_state = lax.map(per_head, (jnp.swapaxes(queries, 0, 1), jnp.swapaxes(keys_values, 0, 1), prior_state, jnp.swapaxes(step_queries, 0, 1), jnp.swapaxes(step_pairs, 0, 1)))
    return (jnp.swapaxes(readout, 0, 1), jnp.swapaxes(decode_out, 0, 1), decode_state)
```

```python
import functools

import jax
import jax.numpy as jnp
from jax import lax
from jax.experimental import pallas as pl
from jax.experimental.pallas import tpu as pltpu
from jax.sharding import PartitionSpec as P

ROOT_TWO = 2.0**0.5
AXIS = "ctx"
VMEM_LIMIT = 56 << 20
IN_VMEM = pl.BlockSpec(memory_space=pltpu.VMEM)
IN_SMEM = pl.BlockSpec(memory_space=pltpu.SMEM)
ANYWHERE = pl.BlockSpec(memory_space=pl.ANY)


def round_up(number, unit):
    return -(-number // unit) * unit


def params():
    return pltpu.CompilerParams(vmem_limit_bytes=VMEM_LIMIT)


def cost(flops, moved):
    return pl.CostEstimate(flops=int(flops), bytes_accessed=int(moved), transcendentals=0)


def swap(value, distance):
    count = lax.axis_size(AXIS)
    return lax.ppermute(value, AXIS, [(one, one ^ distance) for one in range(count)])


def distances(count):
    found = []
    step = count // 2
    while step:
        found.append(step)
        step //= 2
    return found


def gather_all(own, count):
    held = {0: own}
    for step in distances(count):
        held.update({far ^ step: swap(shard, step) for far, shard in list(held.items())})
    return held


def pick_kernel(steps, ids_ref, first_ref, qt_ref, pt_ref, q_ref, p_ref, sems):
    rows = qt_ref.shape[0]
    copies = []
    for step in range(steps):
        spot = jnp.clip(ids_ref[step] - first_ref[0], 0, rows - 1)
        copies.append(
            (
                pltpu.make_async_copy(qt_ref.at[spot], q_ref.at[step], sems.at[0, step]),
                pltpu.make_async_copy(pt_ref.at[spot], p_ref.at[step], sems.at[1, step]),
            )
        )
    for pair in copies:
        for copy in pair:
            copy.start()
    for pair in copies:
        for copy in pair:
            copy.wait()
    for step in range(steps):
        here = ids_ref[step] - first_ref[0]
        outside = jnp.logical_or(here < 0, here >= rows)

        @pl.when(outside)
        def _(step=step):
            q_ref[step] = jnp.zeros(q_ref.shape[1:], q_ref.dtype)
            p_ref[step] = jnp.zeros(p_ref.shape[1:], p_ref.dtype)


def pick_rows(continuation, first, query_table, pair_table):
    steps = continuation.shape[0]
    shapes = [(steps,) + query_table.shape[1:], (steps,) + pair_table.shape[1:]]
    return pl.pallas_call(
        functools.partial(pick_kernel, steps),
        out_shape=[jax.ShapeDtypeStruct(shape, query_table.dtype) for shape in shapes],
        in_specs=[IN_SMEM, IN_SMEM, ANYWHERE, ANYWHERE],
        out_specs=[IN_VMEM, IN_VMEM],
        scratch_shapes=[pltpu.SemaphoreType.DMA((2, steps))],
        compiler_params=params(),
        cost_estimate=cost(0, 8 << 20),
    )(continuation, first, query_table, pair_table)


def turned(value, shift):
    width = value.shape[-1]
    return pltpu.roll(value, lax.rem(2 * width - shift, width), 1)


def feature_block(value, wide, block, first_block):
    partner = turned(value, first_block + block).astype(jnp.float32)
    scale = jnp.float32(ROOT_TWO)
    if block == 0:
        scale = jnp.where(first_block == 0, jnp.float32(1.0), scale)
    return (wide * (partner * scale)).astype(jnp.bfloat16)


def shard_blocks(rows, width, count):
    return max(-(-(rows * at % width + rows) // width) for at in range(count))


def padded_shard(shard, at, blocks):
    rows, width = shard.shape[-2:]
    spot = lax.rem(at * rows, width)
    room = jnp.zeros(shard.shape[:-2] + (blocks * width, width), shard.dtype)
    return lax.dynamic_update_slice_in_dim(room, shard, spot, shard.ndim - 2)


def carry_body(jobs, shard_rows, blocks, aligned, tile, info_ref, ins, outs, phi_ref, state_refs, sems):
    width = phi_ref.shape[-1] // blocks
    copies = {}
    order = []
    for job in jobs:
        key = job[2:4]
        if key not in copies:
            copies[key] = None
            order.append((key, job[4]))
    spots = {}
    for place, (key, slot) in enumerate(order):
        state = state_refs[place]
        source = ins[key[0]]
        if key[1] is not None:
            source = source.at[key[1]]
        if aligned:
            state[:width] = jnp.zeros((width, width), state.dtype)
            state[(blocks - 1) * width :] = jnp.zeros((width, width), state.dtype)
            spot = pl.multiple_of(lax.rem(info_ref[slot] * shard_rows, width), 16)
            target = state.at[pl.ds(spot, shard_rows)]
        else:
            target = state
        copies[key] = pltpu.make_async_copy(source, target, sems.at[place])
        spots[key] = place
        copies[key].start()
    waited = set()
    for query, query_head, state_in, state_head, slot, out, out_head, fresh in jobs:
        key = (state_in, state_head)
        rows = ins[query].shape[1]
        size = min(tile, rows)
        first_block = lax.div(info_ref[slot] * shard_rows, width)

        def expand(at, carry, query=query, query_head=query_head, size=size, first_block=first_block):
            start = pl.multiple_of(at * size, 16)
            value = ins[query][query_head, pl.ds(start, size), :]
            wide = value.astype(jnp.float32)
            for block in range(blocks):
                phi_ref[pl.ds(start, size), block * width : (block + 1) * width] = feature_block(
                    value, wide, block, first_block
                )
            return carry

        lax.fori_loop(0, rows // size, expand, 0)
        if key not in waited:
            copies[key].wait()
            waited.add(key)
        added = jnp.dot(
            phi_ref[:rows], state_refs[spots[key]][...], preferred_element_type=jnp.float32
        )
        if fresh is not None:
            added = added + ins[fresh][out_head]
        elif (out, out_head) in outs["seen"]:
            added = added + outs[out][out_head]
        outs["seen"].add((out, out_head))
        outs[out][out_head] = added
    return None


def carry(jobs, arrays, kinds, outputs, info, shard_rows, blocks, aligned, finish=None):
    width = arrays[0].shape[-1]
    rows = max(arrays[job[0]].shape[1] for job in jobs)
    pieces = len({job[2:4] for job in jobs})
    sums = len(outputs)
    flops = sum(2 * arrays[job[0]].shape[1] * blocks * width * width for job in jobs)

    def kernel(*refs):
        info_ref, refs = refs[0], refs[1:]
        ins = refs[: len(arrays)]
        refs = refs[len(arrays) :]
        results = refs[: len(out_shape)]
        refs = refs[len(out_shape) :]
        if finish is None:
            outs = {at: results[at] for at in range(sums)}
        else:
            outs = {at: refs[at] for at in range(sums)}
            refs = refs[sums:]
        outs["seen"] = set()
        phi_ref, state_refs, sems = refs[0], refs[1:-1], refs[-1]
        carry_body(
            jobs, shard_rows, blocks, aligned, 96, info_ref, ins, outs, phi_ref, state_refs, sems
        )
        if finish is not None:
            finish[1](info_ref, ins, outs, results)

    if finish is None:
        out_shape = [jax.ShapeDtypeStruct(shape, jnp.float32) for shape in outputs]
        held = []
    else:
        out_shape = finish[0]
        held = [pltpu.VMEM(shape, jnp.float32) for shape in outputs]
    return pl.pallas_call(
        kernel,
        out_shape=out_shape,
        in_specs=[IN_SMEM] + [IN_VMEM if kind == "v" else ANYWHERE for kind in kinds],
        out_specs=[IN_VMEM] * len(out_shape),
        scratch_shapes=held
        + [pltpu.VMEM((rows, blocks * width), jnp.bfloat16)]
        + [pltpu.VMEM((blocks * width, width), jnp.bfloat16)] * pieces
        + [pltpu.SemaphoreType.DMA((pieces,))],
        compiler_params=params(),
        cost_estimate=cost(flops * 4, 1 << 20),
    )(info, *arrays)


def squared_sum(query, key, value, allowed=None):
    scores = lax.dot_general(
        query, key, (((1,), (1,)), ((), ())), preferred_element_type=jnp.float32
    )
    weights = scores * scores * (1.0 / query.shape[-1])
    if allowed is not None:
        weights = jnp.where(allowed, weights, 0.0)
    return jnp.dot(weights.astype(jnp.bfloat16), value, preferred_element_type=jnp.float32)


def window_kernel(slots, group, info_ref, q_ref, sq_ref, sp_ref, *refs):
    kv_refs, (own_ref, step_ref) = refs[: len(slots)], refs[len(slots) :]
    me = info_ref[0]
    for head in range(q_ref.shape[0]):
        query = q_ref[head]
        keys = kv_refs[0].shape[2]
        row = lax.broadcasted_iota(jnp.int32, (query.shape[0], keys), 0)
        col = lax.broadcasted_iota(jnp.int32, (query.shape[0], keys), 1)
        own_ref[head] = squared_sum(
            query, kv_refs[0][0, head], kv_refs[0][1, head], col * group <= row
        )
        for place in range(1, len(slots)):

            @pl.when(info_ref[place] < me)
            def _(place=place):
                own_ref[head] += squared_sum(query, kv_refs[place][0, head], kv_refs[place][1, head])

        steps = sq_ref[head]
        step_keys = sp_ref.shape[2]
        row = lax.broadcasted_iota(jnp.int32, (steps.shape[0], step_keys), 0)
        col = lax.broadcasted_iota(jnp.int32, (steps.shape[0], step_keys), 1)
        first = info_ref[len(slots)]
        total = squared_sum(
            steps, sp_ref[0, head], sp_ref[1, head], (col - first) * group <= row
        )
        for place in range(len(slots)):
            total = total + squared_sum(steps, kv_refs[place][0, head], kv_refs[place][1, head])
        step_ref[head] = total


def window_sums(info, query, step_query, step_pairs, pairs, group):
    slots = tuple(sorted(pairs))
    flops = 4 * query.shape[0] * query.shape[1] * query.shape[2] * pairs[0].shape[2] * len(slots)
    return pl.pallas_call(
        functools.partial(window_kernel, slots, group),
        out_shape=[
            jax.ShapeDtypeStruct(query.shape, jnp.float32),
            jax.ShapeDtypeStruct(step_query.shape, jnp.float32),
        ],
        in_specs=[IN_SMEM] + [IN_VMEM] * (3 + len(slots)),
        out_specs=[IN_VMEM] * 2,
        compiler_params=params(),
        cost_estimate=cost(flops * 3, 2 << 20),
    )(info, query, step_query, step_pairs, *[pairs[slot] for slot in slots])


def state_kernel(info_ref, prior_ref, sp_ref, *refs):
    kv_refs, (out_ref, phi_ref, value_ref) = refs[:-3], refs[-3:]
    rows, width = prior_ref.shape[1:]
    blocks = -(-rows // width)
    start = info_ref[0] * rows
    shift, first_block = lax.rem(start, width), lax.div(start, width)
    for head in range(prior_ref.shape[0]):
        at = 0
        for ref in (sp_ref,) + tuple(kv_refs):
            count = ref.shape[2]
            value_ref[at : at + count] = ref[1, head]
            tile = 96 if count % 96 == 0 else count

            def expand(step, carry, ref=ref, at=at, tile=tile):
                value = ref[0, head, pl.ds(pl.multiple_of(step * tile, 16), tile), :]
                wide = value.astype(jnp.float32)
                lane = lax.broadcasted_iota(jnp.int32, wide.shape, 1)
                moved = turned(wide, shift)
                keep = lane < width - shift

                def partner(block):
                    scale = jnp.float32(ROOT_TWO)
                    if block == 0:
                        scale = jnp.where(first_block == 0, jnp.float32(1.0), scale)
                    by = lax.rem(shift + first_block + block, width)
                    return turned(value, by).astype(jnp.float32) * scale

                last = partner(0)
                for block in range(blocks):
                    follow = partner(block + 1)
                    piece = (moved * jnp.where(keep, last, follow)).astype(jnp.bfloat16)
                    last = follow
                    phi_ref[
                        pl.ds(pl.multiple_of(at + step * tile, 16), tile),
                        block * width : (block + 1) * width,
                    ] = piece
                return carry

            lax.fori_loop(0, count // tile, expand, 0)
            at += count
        total = lax.dot_general(
            phi_ref[...],
            value_ref[...],
            (((0,), (0,)), ((), ())),
            preferred_element_type=jnp.float32,
        )
        out_ref[head] = prior_ref[head].astype(jnp.float32) + total[:rows]


def state_rows(info, prior, step_pairs, pairs):
    slots = tuple(sorted(pairs))
    rows, width = prior.shape[1:]
    tokens = step_pairs.shape[2] + sum(pairs[slot].shape[2] for slot in slots)
    return pl.pallas_call(
        state_kernel,
        out_shape=jax.ShapeDtypeStruct(prior.shape, jnp.float32),
        in_specs=[IN_SMEM] + [IN_VMEM] * (2 + len(slots)),
        out_specs=IN_VMEM,
        scratch_shapes=[
            pltpu.VMEM((tokens, round_up(rows, width)), jnp.bfloat16),
            pltpu.VMEM((tokens, width), jnp.bfloat16),
        ],
        compiler_params=params(),
        cost_estimate=cost(8 * prior.shape[0] * rows * width * tokens, 4 << 20),
    )(info, prior, step_pairs, *[pairs[slot] for slot in slots])


def on_device(queries, keys_values, prior_state, counts, continuation, query_table, pair_table):
    tokens, heads, group, width = queries.shape
    count = lax.axis_size(AXIS)
    me = lax.axis_index(AXIS)
    shard_rows = prior_state.shape[1]
    steps = continuation.shape[0]
    own_steps = steps // count
    slots = tuple(range(count))
    aligned = shard_rows % 16 == 0
    blocks = shard_blocks(shard_rows, width, count)

    pairs_own = jnp.transpose(keys_values, (2, 1, 0, 3))
    pairs = gather_all(pairs_own, count)
    priors = [gather_all(prior_state[head], count) for head in range(heads)]

    first = (me * query_table.shape[0]).astype(jnp.int32)[None]
    picked_q, picked_p = pick_rows(
        continuation,
        first,
        jnp.transpose(query_table, (0, 2, 1, 3)),
        pair_table,
    )
    far = distances(count)
    for step in reversed(far[1:]):
        picked_q = picked_q + swap(picked_q, step)
        picked_p = picked_p + swap(picked_p, step)
    if far:
        wanted = lax.dynamic_slice_in_dim(picked_q, (me ^ far[0]) * own_steps, own_steps, 0)
        kept = lax.dynamic_slice_in_dim(picked_q, me * own_steps, own_steps, 0)
        step_q = kept + swap(wanted, far[0])
        step_p = picked_p + swap(picked_p, far[0])
    else:
        step_q, step_p = picked_q, picked_p

    query = jnp.transpose(queries, (1, 0, 2, 3)).reshape(heads, tokens * group, width)
    step_rows = own_steps * group
    step_room = round_up(step_rows, 16)
    step_query = jnp.transpose(step_q, (2, 0, 1, 3)).reshape(heads, step_rows, width)
    step_query = jnp.pad(step_query, ((0, 0), (0, step_room - step_rows), (0, 0)))
    step_pairs = jnp.transpose(step_p, (2, 1, 0, 3))

    info = jnp.stack([me ^ slot for slot in slots] + [me * own_steps, counts[0]]).astype(jnp.int32)

    near = [slot for slot in slots if slot < max(1, count // 2)]
    others = [slot for slot in slots if slot not in near]

    def shard(head, slot):
        value = priors[head][slot]
        return value if aligned else padded_shard(value, me ^ slot, blocks)

    arrays, kinds, jobs = [query], ["v"], []
    for head in range(heads):
        for slot in near:
            jobs.append((0, head, len(arrays), None, slot, 0, head, None))
            arrays.append(shard(head, slot))
            kinds.append("h")
    (sums,) = carry(jobs, arrays, kinds, [query.shape], info, shard_rows, blocks, aligned)

    own_sum, step_sum = window_sums(info, query, step_query, step_pairs, pairs, group)
    decode_state = state_rows(info, prior_state, step_pairs, pairs)

    arrays, kinds, jobs = [step_query], ["v"], []
    for head in range(heads):
        for slot in near:
            jobs.append((0, head, len(arrays), None, slot, 0, head, None))
            arrays.append(shard(head, slot))
            kinds.append("h")
    (step_sums,) = carry(jobs, arrays, kinds, [step_query.shape], info, shard_rows, blocks, aligned)

    readouts, decodes = [], []
    for head in range(heads):
        arrays = [query, step_query, sums, step_sums, own_sum, step_sum]
        kinds = ["v"] * 6
        arrays = [array[head : head + 1] for array in arrays]
        jobs = []
        for slot in others:
            fresh = slot == others[0]
            jobs.append((0, 0, len(arrays), None, slot, 0, 0, 2 if fresh else None))
            jobs.append((1, 0, len(arrays), None, slot, 1, 0, 3 if fresh else None))
            arrays.append(shard(head, slot))
            kinds.append("h")

        def finish(info_ref, ins, outs, results):
            for at, (place, start) in enumerate(
                (
                    (4, info_ref[0] * tokens),
                    (5, count * tokens + info_ref[count]),
                )
            ):
                row = lax.broadcasted_iota(jnp.int32, results[at].shape, 0).astype(jnp.float32)
                token = jnp.floor((row + 0.5) * (1.0 / group))
                position = token + (info_ref[count + 1] + start + 1).astype(jnp.float32)
                total = outs[at][0] * (1.0 / width) + ins[place][0]
                results[at][...] = (total / jnp.sqrt(position)).astype(jnp.bfloat16)

        shapes = [
            jax.ShapeDtypeStruct(query.shape[1:], jnp.bfloat16),
            jax.ShapeDtypeStruct(step_query.shape[1:], jnp.bfloat16),
        ]
        read, decode = carry(
            jobs,
            arrays,
            kinds,
            [(1,) + query.shape[1:], (1,) + step_query.shape[1:]],
            info,
            shard_rows,
            blocks,
            aligned,
            (shapes, finish),
        )
        readouts.append(read)
        decodes.append(decode[:step_rows])
    readout = jnp.stack(readouts, 1).reshape(tokens, group, heads, width)
    decode_out = jnp.stack(decodes, 1).reshape(own_steps, group, heads, width)
    return (
        jnp.transpose(readout, (0, 2, 1, 3)),
        jnp.transpose(decode_out, (0, 2, 1, 3)),
        decode_state,
    )


def solution(mesh):
    in_specs = (
        P(("groups", "ctx"), "head", None, None),
        P(("groups", "ctx"), "head", None, None),
        P(("groups", "head"), "ctx", None),
        P("groups"),
        P("groups"),
        P("ctx", "head", None, None),
        P("ctx", "head", None, None),
    )
    out_specs = (
        P(("groups", "ctx"), "head", None, None),
        P(("groups", "ctx"), "head", None, None),
        P(("groups", "head"), "ctx", None),
    )
    return jax.shard_map(
        on_device, mesh=mesh, in_specs=in_specs, out_specs=out_specs, check_vma=False
    )
```

```python
import functools

import jax
import jax.numpy as jnp
from jax import lax
from jax.experimental import pallas as pl
from jax.experimental.pallas import tpu as pltpu
from jax.sharding import PartitionSpec as P

ROOT_TWO = 2.0**0.5
AXIS = "ctx"
VMEM_LIMIT = 28 << 20
IN_VMEM = pl.BlockSpec(memory_space=pltpu.VMEM)
IN_SMEM = pl.BlockSpec(memory_space=pltpu.SMEM)
ANYWHERE = pl.BlockSpec(memory_space=pl.ANY)
IN_HBM = pl.BlockSpec(memory_space=pltpu.HBM)


def round_up(number, unit):
    return -(-number // unit) * unit


def params(limit=VMEM_LIMIT):
    return pltpu.CompilerParams(vmem_limit_bytes=limit)


def cost():
    return pl.CostEstimate(flops=1 << 10, bytes_accessed=1 << 10, transcendentals=0)


def swap(value, distance):
    count = lax.axis_size(AXIS)
    return lax.ppermute(value, AXIS, [(one, one ^ distance) for one in range(count)])


def distances(count):
    found = []
    step = count // 2
    while step:
        found.append(step)
        step //= 2
    return found


def gather_all(own, steps):
    held = {0: own}
    for step in steps:
        held.update({far ^ step: swap(shard, step) for far, shard in list(held.items())})
    return held


def pick_kernel(info_ref, ids_ref, qt_ref, pt_ref, *refs):
    rows, group = qt_ref.shape[:2]
    outs, sems = refs[:-1], refs[-1]
    steps = outs[0].shape[0]
    first = info_ref[0] * rows

    def targets(step):
        if len(outs) == 2:
            return outs[0].at[step], outs[1].at[step]
        return outs[0].at[step, :group], outs[0].at[step, group:]

    copies = []
    for step in range(steps):
        spot = jnp.clip(ids_ref[step] - first, 0, rows - 1)
        for at, (table, target) in enumerate(zip((qt_ref, pt_ref), targets(step))):
            copies.append(pltpu.make_async_copy(table.at[spot], target, sems.at[at, step]))
    for copy in copies:
        copy.start()
    for copy in copies:
        copy.wait()
    for step in range(steps):
        here = ids_ref[step] - first

        @pl.when(jnp.logical_or(here < 0, here >= rows))
        def _(step=step):
            for out in outs:
                out[step] = jnp.zeros(out.shape[1:], out.dtype)


def pick_rows(info, continuation, query_table, pair_table):
    steps = continuation.shape[0]
    parts = [query_table.shape[1:], pair_table.shape[1:]]
    joined = parts[0][1:] == parts[1][1:]
    if joined:
        parts = [(parts[0][0] + parts[1][0],) + parts[0][1:]]
    found = pl.pallas_call(
        pick_kernel,
        out_shape=[jax.ShapeDtypeStruct((steps,) + part, query_table.dtype) for part in parts],
        in_specs=[IN_SMEM, IN_SMEM, IN_HBM, IN_HBM],
        out_specs=[IN_VMEM] * len(parts),
        scratch_shapes=[pltpu.SemaphoreType.DMA((2, steps))],
        compiler_params=params(52 << 20),
        cost_estimate=cost(),
    )(info, continuation, query_table, pair_table)
    if joined:
        return found[0]
    spare = pair_table.shape[2] - query_table.shape[2]
    padded = jnp.pad(found[0], ((0, 0), (0, 0), (0, spare), (0, 0)))
    return jnp.concatenate([padded, found[1]], 1)


def feature_block(value, wide, block, first_block):
    width = value.shape[-1]
    shift = lax.rem(2 * width - first_block - block, width)
    scale = jnp.float32(ROOT_TWO)
    if block == 0:
        scale = jnp.where(first_block == 0, jnp.float32(1.0), scale)
    partner = pltpu.roll(value, shift, 1).astype(jnp.float32) * scale
    return (wide * partner).astype(jnp.bfloat16)


def feature_pairs(value, blocks, first_block):
    width = value.shape[-1]
    wide = value.astype(jnp.float32)
    for block in range(0, blocks, 2):
        parts = [
            feature_block(value, wide, at, first_block) for at in range(block, min(block + 2, blocks))
        ]
        yield block * width, jnp.concatenate(parts, 1) if len(parts) > 1 else parts[0]


class Span:
    def __init__(self, shards, count, shard_rows, width):
        self.shards, self.rows, self.width = shards, shard_rows, width
        self.total = shards * shard_rows
        self.blocks = max(
            -(-(self.total * at % width + self.total) // width) for at in range(count // shards)
        )
        self.shape = (self.blocks * width, width)
        self.aligned = shard_rows % 16 == 0

    def first_block(self, index):
        return lax.div(lax.div(index, self.shards) * self.total, self.width)

    def spot(self, index):
        at = lax.rem(lax.div(index, self.shards) * self.total, self.width)
        return at + lax.rem(index, self.shards) * self.rows

    def clear(self, ref):
        for edge in (slice(0, self.width), slice(self.shape[0] - self.width, self.shape[0])):
            ref[edge] = jnp.zeros((self.width, self.width), ref.dtype)

    def place(self, source, ref, index, first, sem):
        spot = pl.multiple_of(self.spot(index) + first, 16)
        return pltpu.make_async_copy(source, ref.at[pl.ds(spot, source.shape[0])], sem)

    def room(self, held, me):
        room = jnp.zeros(self.shape, held[0][2].dtype)
        for slot, first, rows in held:
            room = lax.dynamic_update_slice_in_dim(room, rows, self.spot(me ^ slot) + first, 0)
        return room


class States:
    def __init__(self, span, lists):
        self.span, self.arrays, self.plan = span, [], []
        for pieces in lists:
            entry = []
            for array, head, slot, first in pieces:
                if not any(array is one for one in self.arrays):
                    self.arrays.append(array)
                place = [array is one for one in self.arrays].index(True)
                entry.append((place, head, slot, first))
            self.plan.append(entry)

    def scratch(self):
        copies = sum(len(entry) for entry in self.plan)
        return [pltpu.VMEM(self.span.shape, jnp.bfloat16)] * len(self.plan) + [
            pltpu.SemaphoreType.DMA((copies,))
        ]

    def bring(self, refs, scratch, info_ref):
        buffers, sems = scratch[:-1], scratch[-1]
        copies = []
        for buffer, entry in zip(buffers, self.plan):
            if self.span.aligned:
                self.span.clear(buffer)
            for place, head, slot, first in entry:
                source = refs[place] if head is None else refs[place].at[head]
                sem = sems.at[len(copies)]
                if self.span.aligned:
                    copies.append(self.span.place(source, buffer, info_ref[slot], first, sem))
                else:
                    copies.append(pltpu.make_async_copy(source, buffer, sem))
        for copy in copies:
            copy.start()
        return copies


def carried(value, state_ref, span, first_block, out_ref, fresh):
    for start, part in feature_pairs(value, span.blocks, first_block):
        added = jnp.dot(
            part, state_ref[start : start + part.shape[1]], preferred_element_type=jnp.float32
        )
        if fresh and start == 0:
            out_ref[...] = added
        else:
            out_ref[...] += added


def by_head(value):
    return jnp.swapaxes(value, 0, 1)


def near_kernel(span, states, info_ref, q_ref, *refs):
    ins = refs[: len(states.arrays)]
    sum_ref = refs[len(states.arrays)]
    scratch = refs[len(states.arrays) + 1 :]
    copies = states.bring(ins, scratch, info_ref)
    query = by_head(q_ref[...])
    first_block = span.first_block(info_ref[0])
    for copy in copies:
        copy.wait()
    for head in range(query.shape[0]):
        carried(query[head], scratch[head], span, first_block, sum_ref.at[head], True)


def near_sums(info, query, span, states):
    rows, heads, width = query.shape
    return pl.pallas_call(
        functools.partial(near_kernel, span, states),
        out_shape=jax.ShapeDtypeStruct((heads, rows, width), jnp.float32),
        in_specs=[IN_SMEM, IN_VMEM] + [ANYWHERE] * len(states.arrays),
        out_specs=IN_VMEM,
        scratch_shapes=states.scratch(),
        compiler_params=params(),
        cost_estimate=cost(),
    )(info, query, *states.arrays)


def squared_sum(query, keys, values, scale, bound):
    scores = lax.dot_general(
        query, keys, (((1,), (1,)), ((), ())), preferred_element_type=jnp.float32
    )
    row = lax.broadcasted_iota(jnp.int32, scores.shape, 0)
    weights = jnp.where(bound <= row, scores * scores * scale, 0.0).astype(jnp.bfloat16)
    return jnp.dot(weights, values, preferred_element_type=jnp.float32)


def columns(count):
    return lax.broadcasted_iota(jnp.int32, (1, count), 1)


def step_parts(final_ref, heads, step_rows, steps):
    queries = by_head(final_ref[:step_rows])
    pairs = [
        by_head(final_ref[step_rows + head * steps : step_rows + (head + 1) * steps])
        for head in range(heads)
    ]
    return queries, pairs


def keys_kernel(
    slots, group, steps, span, info_ref, q_ref, mine_ref, theirs_ref, prior_ref, near_ref, *refs
):
    kv_refs = refs[:slots]
    sum_ref, step_ref, f_ref, state_ref, rows_ref = refs[slots:]
    f_ref[...] = mine_ref[...] + theirs_ref[...]
    rows, heads, width = q_ref.shape
    step_rows = step_ref.shape[1]
    me = info_ref[0]
    query = by_head(q_ref[...])
    step_query, step_pairs = step_parts(f_ref, heads, step_rows, steps)
    first_block = span.first_block(me)
    keys = kv_refs[0].shape[0]
    unit = 1.0 / width
    for head in range(heads):
        pairs = [by_head(kv_ref[:, head]) for kv_ref in kv_refs]
        total = near_ref[head] * unit
        steps_total = None
        for start in range(0, slots, 4):
            part = pairs[start : start + 4]
            column = columns(len(part) * keys)
            scale = jnp.zeros(column.shape, jnp.float32)
            for at in range(len(part)):
                used = jnp.logical_or(info_ref[start + at] < me, start + at == 0)
                factor = jnp.where(used, jnp.float32(unit), jnp.float32(0.0))
                scale = jnp.where(column >= at * keys, factor, scale)
            bound = jnp.where(column < keys, column * group, 0) if start == 0 else column * 0
            part_keys = jnp.concatenate([pair[0] for pair in part], 0)
            part_values = jnp.concatenate([pair[1] for pair in part], 0)
            total = total + squared_sum(query[head], part_keys, part_values, scale, bound)
            full = jnp.full(column.shape, unit, jnp.float32)
            added = squared_sum(step_query[head], part_keys, part_values, full, column * 0)
            steps_total = added if steps_total is None else steps_total + added
        sum_ref[head] = total
        key, value = step_pairs[head][0], step_pairs[head][1]
        column = columns(steps)
        full = jnp.full(column.shape, unit, jnp.float32)
        step_ref[head] = steps_total + squared_sum(
            step_query[head], key, value, full, (column - info_ref[slots]) * group
        )
        all_keys = jnp.concatenate([pair[0] for pair in pairs] + [key], 0)
        all_values = jnp.concatenate([pair[1] for pair in pairs] + [value], 0)
        turned = all_values.astype(jnp.float32).T.astype(jnp.bfloat16)
        for start, part in feature_pairs(all_keys, span.blocks, first_block):
            added = jnp.dot(turned, part, preferred_element_type=jnp.float32).T
            if span.aligned:
                rows_ref[start : start + part.shape[1]] = added
            else:
                state_ref[head, start : start + part.shape[1]] = added
        if span.aligned:
            spot = pl.multiple_of(span.spot(me), 16)
            state_ref[head] = prior_ref[head].astype(jnp.float32) + rows_ref[pl.ds(spot, span.rows)]


def key_sums(info, query, mine, theirs, prior, near, pairs, step_rows, steps, group, span):
    rows, heads, width = query.shape
    slots = len(pairs)
    state_shape = prior.shape if span.aligned else (heads,) + span.shape
    return pl.pallas_call(
        functools.partial(keys_kernel, slots, group, steps, span),
        out_shape=[
            jax.ShapeDtypeStruct((heads, rows, width), jnp.float32),
            jax.ShapeDtypeStruct((heads, step_rows, width), jnp.float32),
            jax.ShapeDtypeStruct(mine.shape, mine.dtype),
            jax.ShapeDtypeStruct(state_shape, jnp.float32),
        ],
        in_specs=[IN_SMEM] + [IN_VMEM] * (5 + slots),
        out_specs=[IN_VMEM] * 4,
        scratch_shapes=[pltpu.VMEM(span.shape, jnp.float32)],
        compiler_params=params(),
        cost_estimate=cost(),
    )(info, query, mine, theirs, prior, near, *[pairs[slot] for slot in range(slots)])


def far_kernel(head, group, count, tokens, span, states, outputs, info_ref, q_ref, f_ref, *refs):
    ins, refs = refs[: len(states.arrays)], refs[len(states.arrays) :]
    sum_ref, step_ref, refs = refs[0], refs[1], refs[2:]
    taken = 3 if head else 0
    earlier, refs = refs[:taken], refs[taken:]
    results, refs = refs[:outputs], refs[outputs:]
    total_ref, scratch = refs[0], refs[1 : 2 + len(states.plan)]
    rows, heads, width = q_ref.shape
    step_rows = step_ref.shape[1]
    copies = states.bring(ins, scratch, info_ref)
    query = by_head(q_ref[...])
    step_query = by_head(f_ref[:step_rows])
    first_block = span.first_block(info_ref[0])
    far_block = span.first_block(info_ref[count // 2])
    for copy in copies:
        copy.wait()
    both = jnp.concatenate([query[head], step_query[head]], 0)
    carried(both, scratch[len(states.plan) - 1], span, far_block, total_ref, True)
    if head:
        near_ref = earlier[2]
    else:
        near_ref = results[2] if heads > 1 else refs[-1]
        for one in range(heads):
            carried(step_query[one], scratch[one], span, first_block, near_ref.at[one], True)
    start = info_ref[count + 1] + 1
    found = []
    for own, total, first in (
        (sum_ref[head], total_ref[:rows], start + info_ref[0] * tokens),
        (
            step_ref[head],
            total_ref[rows:] + near_ref[head],
            start + count * tokens + info_ref[count],
        ),
    ):
        row = lax.broadcasted_iota(jnp.int32, own.shape, 0).astype(jnp.float32)
        token = jnp.floor((row + 0.5) * (1.0 / group))
        position = token + first.astype(jnp.float32)
        found.append((total * (1.0 / width) + own) / jnp.sqrt(position))
    for at in range(2):
        if head < heads - 1:
            done = [earlier[at][one] for one in range(head)] + [found[at]]
            for one, value in enumerate(done):
                results[at][one] = value
        else:
            done = [earlier[at][one] for one in range(head)] + [found[at]]
            results[at][...] = jnp.stack(done, 1).astype(jnp.bfloat16)


def far_sums(head, info, query, final, sums, step_sums, earlier, group, count, span, states):
    rows, heads, width = query.shape
    step_rows = step_sums.shape[1]
    held = [pltpu.VMEM((rows + step_rows, width), jnp.float32)]
    near = jax.ShapeDtypeStruct((heads, step_rows, width), jnp.float32)
    if head == heads - 1:
        shapes = [
            jax.ShapeDtypeStruct((rows, heads, width), jnp.bfloat16),
            jax.ShapeDtypeStruct((step_rows, heads, width), jnp.bfloat16),
        ]
    else:
        shapes = [
            jax.ShapeDtypeStruct((head + 1, rows, width), jnp.float32),
            jax.ShapeDtypeStruct((head + 1, step_rows, width), jnp.float32),
        ] + ([near] if head == 0 else [])
    spare = [pltpu.VMEM(near.shape, near.dtype)] if heads == 1 else []
    return pl.pallas_call(
        functools.partial(
            far_kernel, head, group, count, rows // group, span, states, len(shapes)
        ),
        out_shape=shapes,
        in_specs=[IN_SMEM]
        + [IN_VMEM] * 2
        + [ANYWHERE] * len(states.arrays)
        + [IN_VMEM] * (2 + len(earlier)),
        out_specs=[IN_VMEM] * len(shapes),
        scratch_shapes=held + states.scratch() + spare,
        compiler_params=params(),
        cost_estimate=cost(),
    )(info, query, final, *states.arrays, sums, step_sums, *earlier)


def on_device(queries, keys_values, prior_state, counts, continuation, query_table, pair_table):
    tokens, heads, group, width = queries.shape
    count = lax.axis_size(AXIS)
    me = lax.axis_index(AXIS)
    shard_rows = prior_state.shape[1]
    steps = continuation.shape[0]
    own_steps = steps // count
    step_rows = own_steps * group
    slots = range(count)
    far, nearer = distances(count)[0], distances(count)[1:]
    info = jnp.stack([me ^ slot for slot in slots] + [me * own_steps, counts[0]]).astype(jnp.int32)

    pairs = gather_all(keys_values, [far] + nearer)
    near_prior = gather_all(prior_state, nearer)

    half = shard_rows // 2
    half = round_up(half, 16) if shard_rows % 16 == 0 else half
    cuts = [(0, half), (half, shard_rows)]
    parts = [(head, first, prior_state[head, first:stop]) for head in range(heads) for first, stop in cuts]
    opening, continuation = lax.optimization_barrier((parts[0][2], continuation))
    parts[0] = (0, 0, opening)

    picked = pick_rows(
        info, continuation, jnp.transpose(query_table, (0, 2, 1, 3)), pair_table
    )
    for step in reversed(nearer):
        picked = picked + swap(picked, step)

    def share(index):
        mine = lax.dynamic_slice_in_dim(picked[:, :group], index * own_steps, own_steps, 0)
        pair = jnp.transpose(picked[:, group:], (1, 0, 2, 3))
        return jnp.concatenate(
            [mine.reshape(step_rows, 2, width), pair.reshape(heads * steps, 2, width)], 0
        )

    outgoing = share(me ^ far)
    mine, theirs = share(me), swap(outgoing, far)
    arrived = [swap(opening, far)]
    for head, first, rows in parts[1:]:
        rows, _ = lax.optimization_barrier((rows, outgoing))
        arrived.append(swap(rows, far))

    def passed_on(at, after):
        head, first, _ = parts[at]
        rows, _ = lax.optimization_barrier((arrived[at], after))
        return [(slot ^ far, first, part) for slot, part in sorted(gather_all(rows, nearer).items())]

    query = jnp.transpose(queries, (0, 2, 1, 3)).reshape(tokens * group, heads, width)
    span = Span(far, count, shard_rows, width)
    own_span = Span(1, count, shard_rows, width)

    def pieces(held, head):
        if span.aligned:
            return [(rows, None if rows.ndim == 2 else head, slot, first) for slot, first, rows in held]
        held = [(slot, first, rows if rows.ndim == 2 else rows[head]) for slot, first, rows in held]
        return [(span.room(held, me), None, 0, 0)]

    near_held = [(slot, 0, rows) for slot, rows in sorted(near_prior.items())]
    near_pieces = [pieces(near_held, head) for head in range(heads)]
    near = near_sums(info, query, span, States(span, near_pieces))
    held = [passed_on(0, near)]
    sums, step_sums, final, decode_state = key_sums(
        info, query, mine, theirs, prior_state, near, pairs, step_rows, steps, group, own_span
    )
    held.append(passed_on(1, sums))
    if not own_span.aligned:
        added = lax.dynamic_slice_in_dim(decode_state, own_span.spot(me), shard_rows, 1)
        decode_state = prior_state.astype(jnp.float32) + added
    earlier = []
    for head in range(heads):
        far_pieces = pieces(held[2 * head] + held[2 * head + 1], head)
        states = States(span, (near_pieces if head == 0 else []) + [far_pieces])
        found = far_sums(
            head, info, query, final, sums, step_sums, earlier, group, count, span, states
        )
        earlier = list(found[:2]) + (earlier[2:] if head else list(found[2:]))
        if head < heads - 1:
            held += [passed_on(2 * head + 2, found[0]), passed_on(2 * head + 3, found[0])]
    readout, decode_out = earlier[:2]
    readout = jnp.transpose(readout.reshape(tokens, group, heads, width), (0, 2, 1, 3))
    decode_out = jnp.transpose(decode_out.reshape(own_steps, group, heads, width), (0, 2, 1, 3))
    return (readout, decode_out, decode_state)


def solution(mesh):
    in_specs = (
        P(("groups", "ctx"), "head", None, None),
        P(("groups", "ctx"), "head", None, None),
        P(("groups", "head"), "ctx", None),
        P("groups"),
        P("groups"),
        P("ctx", "head", None, None),
        P("ctx", "head", None, None),
    )
    out_specs = (
        P(("groups", "ctx"), "head", None, None),
        P(("groups", "ctx"), "head", None, None),
        P(("groups", "head"), "ctx", None),
    )
    return jax.shard_map(
        on_device, mesh=mesh, in_specs=in_specs, out_specs=out_specs, check_vma=False
    )
```

```python
import functools

import jax
import jax.numpy as jnp
from jax import lax
from jax.experimental import pallas as pl
from jax.experimental.pallas import tpu as pltpu
from jax.sharding import PartitionSpec as P

ROOT_TWO = 2.0**0.5
AXIS = "ctx"
VMEM_LIMIT = 28 << 20
IN_VMEM = pl.BlockSpec(memory_space=pltpu.VMEM)
IN_SMEM = pl.BlockSpec(memory_space=pltpu.SMEM)
ANYWHERE = pl.BlockSpec(memory_space=pl.ANY)
IN_HBM = pl.BlockSpec(memory_space=pltpu.HBM)


def round_up(number, unit):
    return -(-number // unit) * unit


def params(limit=VMEM_LIMIT):
    return pltpu.CompilerParams(vmem_limit_bytes=limit)


def cost():
    return pl.CostEstimate(flops=1 << 10, bytes_accessed=1 << 10, transcendentals=0)


def swap(value, distance):
    count = lax.axis_size(AXIS)
    return lax.ppermute(value, AXIS, [(one, one ^ distance) for one in range(count)])


def distances(count):
    found = []
    step = count // 2
    while step:
        found.append(step)
        step //= 2
    return found


def gather_all(own, steps):
    held = {0: own}
    for step in steps:
        held.update({far ^ step: swap(shard, step) for far, shard in list(held.items())})
    return held


def pick_kernel(info_ref, ids_ref, qt_ref, pt_ref, *refs):
    rows, group = qt_ref.shape[:2]
    outs, sems = refs[:-1], refs[-1]
    steps = outs[0].shape[0]
    first = info_ref[0] * rows

    def targets(step):
        if len(outs) == 2:
            return outs[0].at[step], outs[1].at[step]
        return outs[0].at[step, :group], outs[0].at[step, group:]

    copies = []
    for step in range(steps):
        spot = jnp.clip(ids_ref[step] - first, 0, rows - 1)
        for at, (table, target) in enumerate(zip((qt_ref, pt_ref), targets(step))):
            copies.append(pltpu.make_async_copy(table.at[spot], target, sems.at[at, step]))
    for copy in copies:
        copy.start()
    for copy in copies:
        copy.wait()
    for step in range(steps):
        here = ids_ref[step] - first

        @pl.when(jnp.logical_or(here < 0, here >= rows))
        def _(step=step):
            for out in outs:
                out[step] = jnp.zeros(out.shape[1:], out.dtype)


def pick_rows(info, continuation, query_table, pair_table):
    steps = continuation.shape[0]
    parts = [query_table.shape[1:], pair_table.shape[1:]]
    joined = parts[0][1:] == parts[1][1:]
    if joined:
        parts = [(parts[0][0] + parts[1][0],) + parts[0][1:]]
    found = pl.pallas_call(
        pick_kernel,
        out_shape=[jax.ShapeDtypeStruct((steps,) + part, query_table.dtype) for part in parts],
        in_specs=[IN_SMEM, IN_SMEM, IN_HBM, IN_HBM],
        out_specs=[IN_VMEM] * len(parts),
        scratch_shapes=[pltpu.SemaphoreType.DMA((2, steps))],
        compiler_params=params(52 << 20),
        cost_estimate=cost(),
    )(info, continuation, query_table, pair_table)
    if joined:
        return found[0]
    spare = pair_table.shape[2] - query_table.shape[2]
    padded = jnp.pad(found[0], ((0, 0), (0, 0), (0, spare), (0, 0)))
    return jnp.concatenate([padded, found[1]], 1)


def feature_block(value, wide, block, first_block):
    width = value.shape[-1]
    shift = lax.rem(2 * width - first_block - block, width)
    scale = jnp.float32(ROOT_TWO)
    if block == 0:
        scale = jnp.where(first_block == 0, jnp.float32(1.0), scale)
    partner = pltpu.roll(value, shift, 1).astype(jnp.float32) * scale
    return (wide * partner).astype(jnp.bfloat16)


def feature_pairs(value, blocks, first_block):
    width = value.shape[-1]
    wide = value.astype(jnp.float32)
    for block in range(0, blocks, 2):
        parts = [
            feature_block(value, wide, at, first_block) for at in range(block, min(block + 2, blocks))
        ]
        yield block * width, jnp.concatenate(parts, 1) if len(parts) > 1 else parts[0]


class Span:
    def __init__(self, shards, count, shard_rows, width):
        self.shards, self.rows, self.width = shards, shard_rows, width
        self.total = shards * shard_rows
        self.blocks = max(
            -(-(self.total * at % width + self.total) // width) for at in range(count // shards)
        )
        self.shape = (self.blocks * width, width)
        self.aligned = shard_rows % 16 == 0

    def first_block(self, index):
        return lax.div(lax.div(index, self.shards) * self.total, self.width)

    def spot(self, index):
        at = lax.rem(lax.div(index, self.shards) * self.total, self.width)
        return at + lax.rem(index, self.shards) * self.rows

    def clear(self, ref):
        for edge in (slice(0, self.width), slice(self.shape[0] - self.width, self.shape[0])):
            ref[edge] = jnp.zeros((self.width, self.width), ref.dtype)

    def place(self, source, ref, index, first, sem):
        spot = pl.multiple_of(self.spot(index) + first, 16)
        return pltpu.make_async_copy(source, ref.at[pl.ds(spot, source.shape[0])], sem)

    def room(self, held, me):
        room = jnp.zeros(self.shape, held[0][2].dtype)
        for slot, first, rows in held:
            room = lax.dynamic_update_slice_in_dim(room, rows, self.spot(me ^ slot) + first, 0)
        return room


class States:
    def __init__(self, span, lists):
        self.span, self.arrays, self.plan = span, [], []
        for pieces in lists:
            entry = []
            for array, head, slot, first in pieces:
                if not any(array is one for one in self.arrays):
                    self.arrays.append(array)
                place = [array is one for one in self.arrays].index(True)
                entry.append((place, head, slot, first))
            self.plan.append(entry)

    def scratch(self):
        copies = sum(len(entry) for entry in self.plan)
        return [pltpu.VMEM(self.span.shape, jnp.bfloat16)] * len(self.plan) + [
            pltpu.SemaphoreType.DMA((copies,))
        ]

    def bring(self, refs, scratch, info_ref):
        buffers, sems = scratch[:-1], scratch[-1]
        copies = []
        for buffer, entry in zip(buffers, self.plan):
            if self.span.aligned:
                self.span.clear(buffer)
            for place, head, slot, first in entry:
                source = refs[place] if head is None else refs[place].at[head]
                sem = sems.at[len(copies)]
                if self.span.aligned:
                    copies.append(self.span.place(source, buffer, info_ref[slot], first, sem))
                else:
                    copies.append(pltpu.make_async_copy(source, buffer, sem))
        for copy in copies:
            copy.start()
        return copies


def carried(value, state_ref, span, first_block, out_ref, fresh):
    for start, part in feature_pairs(value, span.blocks, first_block):
        added = jnp.dot(
            part, state_ref[start : start + part.shape[1]], preferred_element_type=jnp.float32
        )
        if fresh and start == 0:
            out_ref[...] = added
        else:
            out_ref[...] += added


def by_head(value):
    return jnp.swapaxes(value, 0, 1)


def inverse_root(ref, group, first):
    row = lax.broadcasted_iota(jnp.int32, ref.shape, 0).astype(jnp.float32)
    token = jnp.floor((row + 0.5) * (1.0 / group))
    ref[...] = 1.0 / jnp.sqrt(token + first.astype(jnp.float32))


def near_kernel(span, states, group, count, info_ref, q_ref, *refs):
    ins = refs[: len(states.arrays)]
    sum_ref, by_ref, root_ref, step_root_ref = refs[len(states.arrays) : len(states.arrays) + 4]
    scratch = refs[len(states.arrays) + 4 :]
    copies = states.bring(ins, scratch, info_ref)
    query = by_head(q_ref[...])
    by_ref[...] = query
    tokens = query.shape[1] // group
    start = info_ref[count + 1] + 1
    inverse_root(root_ref, group, start + info_ref[0] * tokens)
    inverse_root(step_root_ref, group, start + count * tokens + info_ref[count])
    first_block = span.first_block(info_ref[0])
    for copy in copies:
        copy.wait()
    for head in range(query.shape[0]):
        carried(query[head], scratch[head], span, first_block, sum_ref.at[head], True)


def near_sums(info, query, span, states, step_rows, group, count):
    rows, heads, width = query.shape
    return pl.pallas_call(
        functools.partial(near_kernel, span, states, group, count),
        out_shape=[
            jax.ShapeDtypeStruct((heads, rows, width), jnp.float32),
            jax.ShapeDtypeStruct((heads, rows, width), query.dtype),
            jax.ShapeDtypeStruct((rows, width), jnp.float32),
            jax.ShapeDtypeStruct((step_rows, width), jnp.float32),
        ],
        in_specs=[IN_SMEM, IN_VMEM] + [ANYWHERE] * len(states.arrays),
        out_specs=[IN_VMEM] * 4,
        scratch_shapes=states.scratch(),
        compiler_params=params(),
        cost_estimate=cost(),
    )(info, query, *states.arrays)


def squared_sum(query, keys, values, scale, bound):
    scores = lax.dot_general(
        query, keys, (((1,), (1,)), ((), ())), preferred_element_type=jnp.float32
    )
    row = lax.broadcasted_iota(jnp.int32, scores.shape, 0)
    weights = jnp.where(bound <= row, scores * scores * scale, 0.0).astype(jnp.bfloat16)
    return jnp.dot(weights, values, preferred_element_type=jnp.float32)


def columns(count):
    return lax.broadcasted_iota(jnp.int32, (1, count), 1)


def step_parts(final_ref, heads, step_rows, steps):
    queries = by_head(final_ref[:step_rows])
    pairs = [
        by_head(final_ref[step_rows + head * steps : step_rows + (head + 1) * steps])
        for head in range(heads)
    ]
    return queries, pairs


def keys_kernel(
    slots, group, steps, span, info_ref, q_ref, mine_ref, theirs_ref, prior_ref, near_ref, *refs
):
    kv_refs = refs[:slots]
    sum_ref, step_ref, f_ref, state_ref, rows_ref = refs[slots:]
    f_ref[...] = mine_ref[...] + theirs_ref[...]
    heads, rows, width = q_ref.shape
    step_rows = step_ref.shape[1]
    me = info_ref[0]
    step_query, step_pairs = step_parts(f_ref, heads, step_rows, steps)
    first_block = span.first_block(me)
    keys = kv_refs[0].shape[0]
    unit = 1.0 / width
    for head in range(heads):
        pairs = [by_head(kv_ref[:, head]) for kv_ref in kv_refs]
        total = near_ref[head] * unit
        steps_total = None
        for start in range(0, slots, 4):
            part = pairs[start : start + 4]
            column = columns(len(part) * keys)
            scale = jnp.zeros(column.shape, jnp.float32)
            for at in range(len(part)):
                used = jnp.logical_or(info_ref[start + at] < me, start + at == 0)
                factor = jnp.where(used, jnp.float32(unit), jnp.float32(0.0))
                scale = jnp.where(column >= at * keys, factor, scale)
            bound = jnp.where(column < keys, column * group, 0) if start == 0 else column * 0
            part_keys = jnp.concatenate([pair[0] for pair in part], 0)
            part_values = jnp.concatenate([pair[1] for pair in part], 0)
            total = total + squared_sum(q_ref[head], part_keys, part_values, scale, bound)
            full = jnp.full(column.shape, unit, jnp.float32)
            added = squared_sum(step_query[head], part_keys, part_values, full, column * 0)
            steps_total = added if steps_total is None else steps_total + added
        sum_ref[head] = total
        key, value = step_pairs[head][0], step_pairs[head][1]
        column = columns(steps)
        full = jnp.full(column.shape, unit, jnp.float32)
        step_ref[head] = steps_total + squared_sum(
            step_query[head], key, value, full, (column - info_ref[slots]) * group
        )
        all_keys = jnp.concatenate([pair[0] for pair in pairs] + [key], 0)
        all_values = jnp.concatenate([pair[1] for pair in pairs] + [value], 0)
        turned = all_values.astype(jnp.float32).T.astype(jnp.bfloat16)
        for start, part in feature_pairs(all_keys, span.blocks, first_block):
            added = jnp.dot(turned, part, preferred_element_type=jnp.float32).T
            if span.aligned:
                rows_ref[start : start + part.shape[1]] = added
            else:
                state_ref[head, start : start + part.shape[1]] = added
        if span.aligned:
            spot = pl.multiple_of(span.spot(me), 16)
            state_ref[head] = prior_ref[head].astype(jnp.float32) + rows_ref[pl.ds(spot, span.rows)]


def key_sums(info, query, mine, theirs, prior, near, pairs, step_rows, steps, group, span):
    heads, rows, width = query.shape
    slots = len(pairs)
    state_shape = prior.shape if span.aligned else (heads,) + span.shape
    return pl.pallas_call(
        functools.partial(keys_kernel, slots, group, steps, span),
        out_shape=[
            jax.ShapeDtypeStruct((heads, rows, width), jnp.float32),
            jax.ShapeDtypeStruct((heads, step_rows, width), jnp.float32),
            jax.ShapeDtypeStruct(mine.shape, mine.dtype),
            jax.ShapeDtypeStruct(state_shape, jnp.float32),
        ],
        in_specs=[IN_SMEM] + [IN_VMEM] * (5 + slots),
        out_specs=[IN_VMEM] * 4,
        scratch_shapes=[pltpu.VMEM(span.shape, jnp.float32)],
        compiler_params=params(),
        cost_estimate=cost(),
    )(info, query, mine, theirs, prior, near, *[pairs[slot] for slot in range(slots)])


def far_kernel(head, count, span, states, outputs, info_ref, q_ref, f_ref, *refs):
    ins, refs = refs[: len(states.arrays)], refs[len(states.arrays) :]
    sum_ref, step_ref, root_ref, step_root_ref = refs[:4]
    refs = refs[4:]
    taken = 3 if head else 0
    earlier, refs = refs[:taken], refs[taken:]
    results, refs = refs[:outputs], refs[outputs:]
    total_ref, scratch = refs[0], refs[1 : 2 + len(states.plan)]
    heads, rows, width = q_ref.shape
    step_rows = step_ref.shape[1]
    copies = states.bring(ins, scratch, info_ref)
    step_query = by_head(f_ref[:step_rows])
    first_block = span.first_block(info_ref[0])
    far_block = span.first_block(info_ref[count // 2])
    for copy in copies:
        copy.wait()
    both = jnp.concatenate([q_ref[head], step_query[head]], 0)
    carried(both, scratch[len(states.plan) - 1], span, far_block, total_ref, True)
    if head:
        near_ref = earlier[2]
    else:
        near_ref = results[2] if heads > 1 else refs[-1]
        for one in range(heads):
            carried(step_query[one], scratch[one], span, first_block, near_ref.at[one], True)
    unit = 1.0 / width
    found = [
        (total_ref[:rows] * unit + sum_ref[head]) * root_ref[...],
        ((total_ref[rows:] + near_ref[head]) * unit + step_ref[head]) * step_root_ref[...],
    ]
    for at in range(2):
        if head < heads - 1:
            done = [earlier[at][one] for one in range(head)] + [found[at]]
            for one, value in enumerate(done):
                results[at][one] = value
        else:
            done = [earlier[at][one] for one in range(head)] + [found[at]]
            results[at][...] = jnp.stack(done, 1).astype(jnp.bfloat16)


def far_sums(head, info, query, final, sums, step_sums, roots, earlier, count, span, states):
    heads, rows, width = query.shape
    step_rows = step_sums.shape[1]
    held = [pltpu.VMEM((rows + step_rows, width), jnp.float32)]
    near = jax.ShapeDtypeStruct((heads, step_rows, width), jnp.float32)
    if head == heads - 1:
        shapes = [
            jax.ShapeDtypeStruct((rows, heads, width), jnp.bfloat16),
            jax.ShapeDtypeStruct((step_rows, heads, width), jnp.bfloat16),
        ]
    else:
        shapes = [
            jax.ShapeDtypeStruct((head + 1, rows, width), jnp.float32),
            jax.ShapeDtypeStruct((head + 1, step_rows, width), jnp.float32),
        ] + ([near] if head == 0 else [])
    spare = [pltpu.VMEM(near.shape, near.dtype)] if heads == 1 else []
    return pl.pallas_call(
        functools.partial(far_kernel, head, count, span, states, len(shapes)),
        out_shape=shapes,
        in_specs=[IN_SMEM]
        + [IN_VMEM] * 2
        + [ANYWHERE] * len(states.arrays)
        + [IN_VMEM] * (4 + len(earlier)),
        out_specs=[IN_VMEM] * len(shapes),
        scratch_shapes=held + states.scratch() + spare,
        compiler_params=params(),
        cost_estimate=cost(),
    )(info, query, final, *states.arrays, sums, step_sums, *roots, *earlier)


def on_device(queries, keys_values, prior_state, counts, continuation, query_table, pair_table):
    tokens, heads, group, width = queries.shape
    count = lax.axis_size(AXIS)
    me = lax.axis_index(AXIS)
    shard_rows = prior_state.shape[1]
    steps = continuation.shape[0]
    own_steps = steps // count
    step_rows = own_steps * group
    slots = range(count)
    far, nearer = distances(count)[0], distances(count)[1:]
    info = jnp.stack([me ^ slot for slot in slots] + [me * own_steps, counts[0]]).astype(jnp.int32)

    pairs = gather_all(keys_values, [far] + nearer)
    near_prior = gather_all(prior_state, nearer)

    parts = [prior_state[head] for head in range(heads)]
    opening, _ = lax.optimization_barrier((parts[0], pairs[far]))
    arrived = [swap(opening, far)]
    continuation, _ = lax.optimization_barrier((continuation, parts))

    picked = pick_rows(
        info, continuation, jnp.transpose(query_table, (0, 2, 1, 3)), pair_table
    )
    for step in reversed(nearer):
        picked = picked + swap(picked, step)

    def share(index):
        mine = lax.dynamic_slice_in_dim(picked[:, :group], index * own_steps, own_steps, 0)
        pair = jnp.transpose(picked[:, group:], (1, 0, 2, 3))
        return jnp.concatenate(
            [mine.reshape(step_rows, 2, width), pair.reshape(heads * steps, 2, width)], 0
        )

    outgoing = share(me ^ far)
    mine, theirs = share(me), swap(outgoing, far)
    for rows in parts[1:]:
        rows, _ = lax.optimization_barrier((rows, outgoing))
        arrived.append(swap(rows, far))

    def passed_on(head, after):
        rows, _ = lax.optimization_barrier((arrived[head], after))
        return [(slot ^ far, 0, part) for slot, part in sorted(gather_all(rows, nearer).items())]

    query = jnp.transpose(queries, (0, 2, 1, 3)).reshape(tokens * group, heads, width)
    span = Span(far, count, shard_rows, width)
    own_span = Span(1, count, shard_rows, width)

    def pieces(held, head):
        if span.aligned:
            return [(rows, None if rows.ndim == 2 else head, slot, first) for slot, first, rows in held]
        held = [(slot, first, rows if rows.ndim == 2 else rows[head]) for slot, first, rows in held]
        return [(span.room(held, me), None, 0, 0)]

    near_held = [(slot, 0, rows) for slot, rows in sorted(near_prior.items())]
    near_pieces = [pieces(near_held, head) for head in range(heads)]
    query, pairs = lax.optimization_barrier((query, pairs))
    near, query, *roots = near_sums(
        info, query, span, States(span, near_pieces), step_rows, group, count
    )
    sums, step_sums, final, decode_state = key_sums(
        info, query, mine, theirs, prior_state, near, pairs, step_rows, steps, group, own_span
    )
    held = [passed_on(0, (near, theirs))]
    if not own_span.aligned:
        added = lax.dynamic_slice_in_dim(decode_state, own_span.spot(me), shard_rows, 1)
        decode_state = prior_state.astype(jnp.float32) + added
    earlier = []
    for head in range(heads):
        far_pieces = pieces(held[head], head)
        states = States(span, (near_pieces if head == 0 else []) + [far_pieces])
        found = far_sums(
            head, info, query, final, sums, step_sums, roots, earlier, count, span, states
        )
        earlier = list(found[:2]) + (earlier[2:] if head else list(found[2:]))
        if head < heads - 1:
            held.append(passed_on(head + 1, found[0]))
    readout, decode_out = earlier[:2]
    readout = jnp.transpose(readout.reshape(tokens, group, heads, width), (0, 2, 1, 3))
    decode_out = jnp.transpose(decode_out.reshape(own_steps, group, heads, width), (0, 2, 1, 3))
    return (readout, decode_out, decode_state)


def solution(mesh):
    in_specs = (
        P(("groups", "ctx"), "head", None, None),
        P(("groups", "ctx"), "head", None, None),
        P(("groups", "head"), "ctx", None),
        P("groups"),
        P("groups"),
        P("ctx", "head", None, None),
        P("ctx", "head", None, None),
    )
    out_specs = (
        P(("groups", "ctx"), "head", None, None),
        P(("groups", "ctx"), "head", None, None),
        P(("groups", "head"), "ctx", None),
    )
    return jax.shard_map(
        on_device, mesh=mesh, in_specs=in_specs, out_specs=out_specs, check_vma=False
    )
```

```python
import functools

import jax
import jax.numpy as jnp
from jax import lax
from jax.experimental import pallas as pl
from jax.experimental.pallas import tpu as pltpu
from jax.sharding import PartitionSpec as P

ROOT_TWO = 2.0**0.5
AXIS = "ctx"
VMEM_LIMIT = 28 << 20
IN_VMEM = pl.BlockSpec(memory_space=pltpu.VMEM)
IN_SMEM = pl.BlockSpec(memory_space=pltpu.SMEM)
ANYWHERE = pl.BlockSpec(memory_space=pl.ANY)
IN_HBM = pl.BlockSpec(memory_space=pltpu.HBM)


def round_up(number, unit):
    return -(-number // unit) * unit


def params(limit=VMEM_LIMIT):
    return pltpu.CompilerParams(vmem_limit_bytes=limit)


def cost():
    return pl.CostEstimate(flops=1 << 10, bytes_accessed=1 << 10, transcendentals=0)


def swap(value, distance):
    count = lax.axis_size(AXIS)
    return lax.ppermute(value, AXIS, [(one, one ^ distance) for one in range(count)])


def distances(count):
    found = []
    step = count // 2
    while step:
        found.append(step)
        step //= 2
    return found


def gather_all(own, steps):
    held = {0: own}
    for step in steps:
        held.update({far ^ step: swap(shard, step) for far, shard in list(held.items())})
    return held


def pick_kernel(info_ref, ids_ref, qt_ref, pt_ref, *refs):
    rows, group = qt_ref.shape[:2]
    outs, sems = refs[:-1], refs[-1]
    steps = outs[0].shape[0]
    first = info_ref[0] * rows

    def targets(step):
        if len(outs) == 2:
            return outs[0].at[step], outs[1].at[step]
        return outs[0].at[step, :group], outs[0].at[step, group:]

    copies = []
    for step in range(steps):
        spot = jnp.clip(ids_ref[step] - first, 0, rows - 1)
        for at, (table, target) in enumerate(zip((qt_ref, pt_ref), targets(step))):
            copies.append(pltpu.make_async_copy(table.at[spot], target, sems.at[at, step]))
    for copy in copies:
        copy.start()
    for copy in copies:
        copy.wait()
    for step in range(steps):
        here = ids_ref[step] - first

        @pl.when(jnp.logical_or(here < 0, here >= rows))
        def _(step=step):
            for out in outs:
                out[step] = jnp.zeros(out.shape[1:], out.dtype)


def pick_rows(info, continuation, query_table, pair_table):
    steps = continuation.shape[0]
    parts = [query_table.shape[1:], pair_table.shape[1:]]
    joined = parts[0][1:] == parts[1][1:]
    if joined:
        parts = [(parts[0][0] + parts[1][0],) + parts[0][1:]]
    found = pl.pallas_call(
        pick_kernel,
        out_shape=[jax.ShapeDtypeStruct((steps,) + part, query_table.dtype) for part in parts],
        in_specs=[IN_SMEM, IN_SMEM, IN_HBM, IN_HBM],
        out_specs=[IN_VMEM] * len(parts),
        scratch_shapes=[pltpu.SemaphoreType.DMA((2, steps))],
        compiler_params=params(52 << 20),
        cost_estimate=cost(),
    )(info, continuation, query_table, pair_table)
    if joined:
        return found[0]
    spare = pair_table.shape[2] - query_table.shape[2]
    padded = jnp.pad(found[0], ((0, 0), (0, 0), (0, spare), (0, 0)))
    return jnp.concatenate([padded, found[1]], 1)


def feature_block(value, wide, block, first_block):
    width = value.shape[-1]
    shift = lax.rem(2 * width - first_block - block, width)
    scale = jnp.float32(ROOT_TWO)
    if block == 0:
        scale = jnp.where(first_block == 0, jnp.float32(1.0), scale)
    partner = pltpu.roll(value, shift, 1).astype(jnp.float32) * scale
    return (wide * partner).astype(jnp.bfloat16)


def feature_pairs(value, blocks, first_block):
    width = value.shape[-1]
    wide = value.astype(jnp.float32)
    for block in range(0, blocks, 2):
        parts = [
            feature_block(value, wide, at, first_block) for at in range(block, min(block + 2, blocks))
        ]
        yield block * width, jnp.concatenate(parts, 1) if len(parts) > 1 else parts[0]


class Span:
    def __init__(self, shards, count, shard_rows, width):
        self.shards, self.rows, self.width = shards, shard_rows, width
        self.total = shards * shard_rows
        self.blocks = max(
            -(-(self.total * at % width + self.total) // width) for at in range(count // shards)
        )
        self.shape = (self.blocks * width, width)
        self.aligned = shard_rows % 16 == 0

    def first_block(self, index):
        return lax.div(lax.div(index, self.shards) * self.total, self.width)

    def spot(self, index):
        at = lax.rem(lax.div(index, self.shards) * self.total, self.width)
        return at + lax.rem(index, self.shards) * self.rows

    def clear(self, ref):
        for edge in (slice(0, self.width), slice(self.shape[0] - self.width, self.shape[0])):
            ref[edge] = jnp.zeros((self.width, self.width), ref.dtype)

    def place(self, source, ref, index, first, sem):
        spot = pl.multiple_of(self.spot(index) + first, 16)
        return pltpu.make_async_copy(source, ref.at[pl.ds(spot, source.shape[0])], sem)

    def room(self, held, me):
        room = jnp.zeros(self.shape, held[0][2].dtype)
        for slot, first, rows in held:
            room = lax.dynamic_update_slice_in_dim(room, rows, self.spot(me ^ slot) + first, 0)
        return room


class States:
    def __init__(self, span, lists):
        self.span, self.arrays, self.plan = span, [], []
        for pieces in lists:
            entry = []
            for array, head, slot, first in pieces:
                if not any(array is one for one in self.arrays):
                    self.arrays.append(array)
                place = [array is one for one in self.arrays].index(True)
                entry.append((place, head, slot, first))
            self.plan.append(entry)

    def scratch(self):
        copies = sum(len(entry) for entry in self.plan)
        return [pltpu.VMEM(self.span.shape, jnp.bfloat16)] * len(self.plan) + [
            pltpu.SemaphoreType.DMA((copies,))
        ]

    def bring(self, refs, scratch, info_ref):
        buffers, sems = scratch[:-1], scratch[-1]
        copies = []
        for buffer, entry in zip(buffers, self.plan):
            if self.span.aligned:
                self.span.clear(buffer)
            for place, head, slot, first in entry:
                source = refs[place] if head is None else refs[place].at[head]
                sem = sems.at[len(copies)]
                if self.span.aligned:
                    copies.append(self.span.place(source, buffer, info_ref[slot], first, sem))
                else:
                    copies.append(pltpu.make_async_copy(source, buffer, sem))
        for copy in copies:
            copy.start()
        return copies


def carried(value, state_ref, span, first_block, out_ref, fresh):
    for start, part in feature_pairs(value, span.blocks, first_block):
        added = jnp.dot(
            part, state_ref[start : start + part.shape[1]], preferred_element_type=jnp.float32
        )
        if fresh and start == 0:
            out_ref[...] = added
        else:
            out_ref[...] += added


def by_head(value):
    return jnp.swapaxes(value, 0, 1)


def inverse_root(ref, group, first):
    row = lax.broadcasted_iota(jnp.int32, ref.shape, 0).astype(jnp.float32)
    token = jnp.floor((row + 0.5) * (1.0 / group))
    ref[...] = 1.0 / jnp.sqrt(token + first.astype(jnp.float32))


def near_kernel(span, states, group, count, info_ref, q_ref, *refs):
    ins = refs[: len(states.arrays)]
    sum_ref, by_ref, root_ref, step_root_ref = refs[len(states.arrays) : len(states.arrays) + 4]
    scratch = refs[len(states.arrays) + 4 :]
    copies = states.bring(ins, scratch, info_ref)
    query = by_head(q_ref[...])
    by_ref[...] = query
    tokens = query.shape[1] // group
    start = info_ref[count + 1] + 1
    inverse_root(root_ref, group, start + info_ref[0] * tokens)
    inverse_root(step_root_ref, group, start + count * tokens + info_ref[count])
    first_block = span.first_block(info_ref[0])
    for copy in copies:
        copy.wait()
    for head in range(query.shape[0]):
        carried(query[head], scratch[head], span, first_block, sum_ref.at[head], True)


def near_sums(info, query, span, states, step_rows, group, count):
    rows, heads, width = query.shape
    return pl.pallas_call(
        functools.partial(near_kernel, span, states, group, count),
        out_shape=[
            jax.ShapeDtypeStruct((heads, rows, width), jnp.float32),
            jax.ShapeDtypeStruct((heads, rows, width), query.dtype),
            jax.ShapeDtypeStruct((rows, width), jnp.float32),
            jax.ShapeDtypeStruct((step_rows, width), jnp.float32),
        ],
        in_specs=[IN_SMEM, IN_VMEM] + [ANYWHERE] * len(states.arrays),
        out_specs=[IN_VMEM] * 4,
        scratch_shapes=states.scratch(),
        compiler_params=params(),
        cost_estimate=cost(),
    )(info, query, *states.arrays)


def squared_sum(query, keys, values, scale, bound):
    scores = lax.dot_general(
        query, keys, (((1,), (1,)), ((), ())), preferred_element_type=jnp.float32
    )
    row = lax.broadcasted_iota(jnp.int32, scores.shape, 0)
    weights = jnp.where(bound <= row, scores * scores * scale, 0.0).astype(jnp.bfloat16)
    return jnp.dot(weights, values, preferred_element_type=jnp.float32)


def columns(count):
    return lax.broadcasted_iota(jnp.int32, (1, count), 1)


def step_parts(final_ref, heads, step_rows, steps):
    queries = by_head(final_ref[:step_rows])
    pairs = [
        by_head(final_ref[step_rows + head * steps : step_rows + (head + 1) * steps])
        for head in range(heads)
    ]
    return queries, pairs


def keys_kernel(
    slots, group, steps, span, info_ref, q_ref, mine_ref, theirs_ref, prior_ref, near_ref, *refs
):
    kv_refs = refs[:slots]
    sum_ref, step_ref, f_ref, state_ref, rows_ref = refs[slots:]
    f_ref[...] = mine_ref[...] + theirs_ref[...]
    heads, rows, width = q_ref.shape
    step_rows = step_ref.shape[1]
    me = info_ref[0]
    step_query, step_pairs = step_parts(f_ref, heads, step_rows, steps)
    first_block = span.first_block(me)
    keys = kv_refs[0].shape[0]
    unit = 1.0 / width
    for head in range(heads):
        pairs = [by_head(kv_ref[:, head]) for kv_ref in kv_refs]
        total = near_ref[head] * unit
        steps_total = None
        for start in range(0, slots, 4):
            part = pairs[start : start + 4]
            column = columns(len(part) * keys)
            scale = jnp.zeros(column.shape, jnp.float32)
            for at in range(len(part)):
                used = jnp.logical_or(info_ref[start + at] < me, start + at == 0)
                factor = jnp.where(used, jnp.float32(unit), jnp.float32(0.0))
                scale = jnp.where(column >= at * keys, factor, scale)
            bound = jnp.where(column < keys, column * group, 0) if start == 0 else column * 0
            part_keys = jnp.concatenate([pair[0] for pair in part], 0)
            part_values = jnp.concatenate([pair[1] for pair in part], 0)
            total = total + squared_sum(q_ref[head], part_keys, part_values, scale, bound)
            full = jnp.full(column.shape, unit, jnp.float32)
            added = squared_sum(step_query[head], part_keys, part_values, full, column * 0)
            steps_total = added if steps_total is None else steps_total + added
        sum_ref[head] = total
        key, value = step_pairs[head][0], step_pairs[head][1]
        column = columns(steps)
        full = jnp.full(column.shape, unit, jnp.float32)
        step_ref[head] = steps_total + squared_sum(
            step_query[head], key, value, full, (column - info_ref[slots]) * group
        )
        all_keys = jnp.concatenate([pair[0] for pair in pairs] + [key], 0)
        all_values = jnp.concatenate([pair[1] for pair in pairs] + [value], 0)
        turned = all_values.astype(jnp.float32).T.astype(jnp.bfloat16)
        for start, part in feature_pairs(all_keys, span.blocks, first_block):
            added = jnp.dot(turned, part, preferred_element_type=jnp.float32).T
            if span.aligned:
                rows_ref[start : start + part.shape[1]] = added
            else:
                state_ref[head, start : start + part.shape[1]] = added
        if span.aligned:
            spot = pl.multiple_of(span.spot(me), 16)
            state_ref[head] = prior_ref[head].astype(jnp.float32) + rows_ref[pl.ds(spot, span.rows)]


def key_sums(info, query, mine, theirs, prior, near, pairs, step_rows, steps, group, span):
    heads, rows, width = query.shape
    slots = len(pairs)
    state_shape = prior.shape if span.aligned else (heads,) + span.shape
    return pl.pallas_call(
        functools.partial(keys_kernel, slots, group, steps, span),
        out_shape=[
            jax.ShapeDtypeStruct((heads, rows, width), jnp.float32),
            jax.ShapeDtypeStruct((heads, step_rows, width), jnp.float32),
            jax.ShapeDtypeStruct(mine.shape, mine.dtype),
            jax.ShapeDtypeStruct(state_shape, jnp.float32),
        ],
        in_specs=[IN_SMEM] + [IN_VMEM] * (5 + slots),
        out_specs=[IN_VMEM] * 4,
        scratch_shapes=[pltpu.VMEM(span.shape, jnp.float32)],
        compiler_params=params(),
        cost_estimate=cost(),
    )(info, query, mine, theirs, prior, near, *[pairs[slot] for slot in range(slots)])


def far_kernel(head, count, span, states, outputs, info_ref, q_ref, f_ref, *refs):
    ins, refs = refs[: len(states.arrays)], refs[len(states.arrays) :]
    sum_ref, step_ref, root_ref, step_root_ref = refs[:4]
    refs = refs[4:]
    taken = 3 if head else 0
    earlier, refs = refs[:taken], refs[taken:]
    results, refs = refs[:outputs], refs[outputs:]
    total_ref, scratch = refs[0], refs[1 : 2 + len(states.plan)]
    heads, rows, width = q_ref.shape
    step_rows = step_ref.shape[1]
    copies = states.bring(ins, scratch, info_ref)
    step_query = by_head(f_ref[:step_rows])
    first_block = span.first_block(info_ref[0])
    far_block = span.first_block(info_ref[count // 2])
    for copy in copies:
        copy.wait()
    both = jnp.concatenate([q_ref[head], step_query[head]], 0)
    carried(both, scratch[len(states.plan) - 1], span, far_block, total_ref, True)
    if head:
        near_ref = earlier[2]
    else:
        near_ref = results[2] if heads > 1 else refs[-1]
        for one in range(heads):
            carried(step_query[one], scratch[one], span, first_block, near_ref.at[one], True)
    unit = 1.0 / width
    found = [
        (total_ref[:rows] * unit + sum_ref[head]) * root_ref[...],
        ((total_ref[rows:] + near_ref[head]) * unit + step_ref[head]) * step_root_ref[...],
    ]
    for at in range(2):
        if head < heads - 1:
            done = [earlier[at][one] for one in range(head)] + [found[at]]
            for one, value in enumerate(done):
                results[at][one] = value
        else:
            done = [earlier[at][one] for one in range(head)] + [found[at]]
            results[at][...] = jnp.stack(done, 1).astype(jnp.bfloat16)


def far_sums(head, info, query, final, sums, step_sums, roots, earlier, count, span, states):
    heads, rows, width = query.shape
    step_rows = step_sums.shape[1]
    held = [pltpu.VMEM((rows + step_rows, width), jnp.float32)]
    near = jax.ShapeDtypeStruct((heads, step_rows, width), jnp.float32)
    if head == heads - 1:
        shapes = [
            jax.ShapeDtypeStruct((rows, heads, width), jnp.bfloat16),
            jax.ShapeDtypeStruct((step_rows, heads, width), jnp.bfloat16),
        ]
    else:
        shapes = [
            jax.ShapeDtypeStruct((head + 1, rows, width), jnp.float32),
            jax.ShapeDtypeStruct((head + 1, step_rows, width), jnp.float32),
        ] + ([near] if head == 0 else [])
    spare = [pltpu.VMEM(near.shape, near.dtype)] if heads == 1 else []
    return pl.pallas_call(
        functools.partial(far_kernel, head, count, span, states, len(shapes)),
        out_shape=shapes,
        in_specs=[IN_SMEM]
        + [IN_VMEM] * 2
        + [ANYWHERE] * len(states.arrays)
        + [IN_VMEM] * (4 + len(earlier)),
        out_specs=[IN_VMEM] * len(shapes),
        scratch_shapes=held + states.scratch() + spare,
        compiler_params=params(),
        cost_estimate=cost(),
    )(info, query, final, *states.arrays, sums, step_sums, *roots, *earlier)


def on_device(queries, keys_values, prior_state, counts, continuation, query_table, pair_table):
    tokens, heads, group, width = queries.shape
    count = lax.axis_size(AXIS)
    me = lax.axis_index(AXIS)
    shard_rows = prior_state.shape[1]
    steps = continuation.shape[0]
    own_steps = steps // count
    step_rows = own_steps * group
    slots = range(count)
    far, nearer = distances(count)[0], distances(count)[1:]
    info = jnp.stack([me ^ slot for slot in slots] + [me * own_steps, counts[0]]).astype(jnp.int32)

    pairs = gather_all(keys_values, [far] + nearer)
    near_prior = gather_all(prior_state, nearer)

    opening = prior_state[0]
    continuation, _ = lax.optimization_barrier((continuation, (opening, near_prior)))
    opening, _ = lax.optimization_barrier((opening, pairs[far]))
    arrived = [swap(opening, far)]

    picked = pick_rows(
        info, continuation, jnp.transpose(query_table, (0, 2, 1, 3)), pair_table
    )
    for step in reversed(nearer):
        picked = picked + swap(picked, step)

    def share(index):
        mine = lax.dynamic_slice_in_dim(picked[:, :group], index * own_steps, own_steps, 0)
        pair = jnp.transpose(picked[:, group:], (1, 0, 2, 3))
        return jnp.concatenate(
            [mine.reshape(step_rows, 2, width), pair.reshape(heads * steps, 2, width)], 0
        )

    outgoing = share(me ^ far)
    mine, theirs = share(me), swap(outgoing, far)
    rest, _ = lax.optimization_barrier((prior_state, outgoing))
    rest = [rest[head] for head in range(1, heads)]

    def passed_on(head, after):
        rows, _ = lax.optimization_barrier((arrived[head], after))
        return [(slot ^ far, 0, part) for slot, part in sorted(gather_all(rows, nearer).items())]

    query = jnp.transpose(queries, (0, 2, 1, 3)).reshape(tokens * group, heads, width)
    span = Span(far, count, shard_rows, width)
    own_span = Span(1, count, shard_rows, width)

    def pieces(held, head):
        if span.aligned:
            return [(rows, None if rows.ndim == 2 else head, slot, first) for slot, first, rows in held]
        held = [(slot, first, rows if rows.ndim == 2 else rows[head]) for slot, first, rows in held]
        return [(span.room(held, me), None, 0, 0)]

    near_held = [(slot, 0, rows) for slot, rows in sorted(near_prior.items())]
    near_pieces = [pieces(near_held, head) for head in range(heads)]
    query, pairs, rest = lax.optimization_barrier((query, pairs, rest))
    arrived += [swap(rows, far) for rows in rest]
    near, query, *roots = near_sums(
        info, query, span, States(span, near_pieces), step_rows, group, count
    )
    sums, step_sums, final, decode_state = key_sums(
        info, query, mine, theirs, prior_state, near, pairs, step_rows, steps, group, own_span
    )
    held = [passed_on(0, (near, theirs))]
    if not own_span.aligned:
        added = lax.dynamic_slice_in_dim(decode_state, own_span.spot(me), shard_rows, 1)
        decode_state = prior_state.astype(jnp.float32) + added
    earlier = []
    for head in range(heads):
        far_pieces = pieces(held[head], head)
        states = States(span, (near_pieces if head == 0 else []) + [far_pieces])
        found = far_sums(
            head, info, query, final, sums, step_sums, roots, earlier, count, span, states
        )
        earlier = list(found[:2]) + (earlier[2:] if head else list(found[2:]))
        if head < heads - 1:
            held.append(passed_on(head + 1, found[0]))
    readout, decode_out = earlier[:2]
    readout = jnp.transpose(readout.reshape(tokens, group, heads, width), (0, 2, 1, 3))
    decode_out = jnp.transpose(decode_out.reshape(own_steps, group, heads, width), (0, 2, 1, 3))
    return (readout, decode_out, decode_state)


def solution(mesh):
    in_specs = (
        P(("groups", "ctx"), "head", None, None),
        P(("groups", "ctx"), "head", None, None),
        P(("groups", "head"), "ctx", None),
        P("groups"),
        P("groups"),
        P("ctx", "head", None, None),
        P("ctx", "head", None, None),
    )
    out_specs = (
        P(("groups", "ctx"), "head", None, None),
        P(("groups", "ctx"), "head", None, None),
        P(("groups", "head"), "ctx", None),
    )
    return jax.shard_map(
        on_device, mesh=mesh, in_specs=in_specs, out_specs=out_specs, check_vma=False
    )
```
